32 devices in a mesh: groups: 2 (over x), wide: 16 (over z, y, core).
Axes of the slice: x: 2, y: 2, z: 4, core: 2. Of those that a mesh axis runs over, the one named last changes fastest.
Arguments:
- gate_pre: bfloat16 [1024, 32768], P('groups', 'wide'), parts along dimension 0, may hold values from -8 to 8
- up_pre: bfloat16 [1024, 32768], P('groups', 'wide'), parts along dimension 0, may hold values from -8 to 8
- down_weight: bfloat16 [32768, 8192], P('wide'), may hold values from -0.03125 to 0.03125
Outputs:
- block_out: bfloat16 [1024, 8192], P(('groups', 'wide')), parts along dimension 0
The draws below stay inside these ranges and needn't reach their ends.
There are 2 independent parts, one for each index of `groups`. The reference program is written for one: setup_inputs(seed, part) draws one part's arguments, and reference() takes and returns one part's arrays. A program takes and returns all parts, laid end to end along the dimension named above; an argument that names none is the same for every part. Nothing has to cross between parts.
All inputs are finite; a program needn't handle non-finite values.
Results may differ from the reference program's by a relative error of at most 0.005.
Values may be sent and summed in bfloat16 or wider, within the bound.
A program may use at most 128 MiB of HBM per device.

```python
import jax
import jax.numpy as jnp

D_W = 8192
FF_W = 32768
TOKENS = 512


def strengthened(drawn, own_key, source, target, blocks, factor):
    def block_of(dim):
        return (jnp.arange(drawn.shape[dim]) // (drawn.shape[dim] // blocks)).reshape((-1,) + (1,) * (drawn.ndim - 1 - dim))

    one_side = jax.random.permutation(own_key, blocks)[block_of(target)]
    far = (block_of(target) + blocks // 2) % blocks
    return jnp.where((block_of(source) == one_side) | (block_of(source) == far), factor * drawn, drawn)


def levels(key, dims, split, least, top_value):
    loudness, own = 1.0, jax.random.fold_in(key, 6)
    for axis_at, shards_of in split:
        draws = jnp.exp(jax.random.uniform(jax.random.fold_in(own, axis_at), (shards_of,), jnp.float32, least / len(split), top_value / len(split)))
        loudness = loudness * jnp.repeat(draws, dims[axis_at] // shards_of).reshape([-1 if axis == axis_at else 1 for axis in range(len(dims))])
    return loudness


def bell_draw(stream_key, shape, deviation, reach, split=(), dtype=jnp.bfloat16):
    drawn = jax.random.normal(stream_key, shape, jnp.float32) * deviation
    if len(split) > 0:
        drawn = levels(stream_key, shape, split, -0.22, 0.18) * drawn
    return jnp.clip(drawn, min=-reach, max=reach).astype(dtype)


def gaussian_with(stream_key, extent, width, bound, shards, heavy, dtype=jnp.bfloat16):
    entries = width * jax.random.normal(stream_key, extent, jnp.float32)
    if shards:
        entries = entries * levels(stream_key, extent, shards, -0.22, 0.18)
    return jnp.clip(strengthened(entries, jax.random.fold_in(stream_key, 3), *heavy), -bound, bound).astype(dtype)


def setup_inputs(seed: int = 0, part: int = 0) -> dict:
    streams_of = jax.random.split(jax.random.key(seed), 4)
    part_splits = jax.random.split(jax.random.fold_in(streams_of[3], part), 4)
    return {
        "gate_pre": bell_draw(part_splits[0], (TOKENS, FF_W), 1.5, 8.0, ((1, 16),)),
        "up_pre": gaussian_with(part_splits[1], (TOKENS, FF_W), 1.0, 8.0, ((1, 16),), (1, 0, 16, 2.0)),
        "down_weight": bell_draw(streams_of[2], (FF_W, D_W), FF_W ** -0.5, 0.03125, ((0, 16),)),
    }


def reference(gate_pre, up_pre, down_weight):
    hidden = (jax.nn.silu(gate_pre.astype(jnp.float32)) * up_pre.astype(jnp.float32)).astype(jnp.bfloat16)
    return jnp.dot(hidden, down_weight, preferred_element_type=jnp.float32).astype(jnp.bfloat16)
```

```python
import functools

import jax
import jax.numpy as jnp
from jax import lax
from jax.experimental import pallas as pl
from jax.experimental.pallas import tpu as pltpu
from jax.sharding import PartitionSpec as P

MESH = pl.DeviceIdType.MESH
BF16 = jnp.bfloat16
F32 = jnp.float32

ZS = 4
WIDE = 4 * ZS
CHUNK = 512
SLOTS = 3


def plain_per_device(gate_pre, up_pre, down_weight):
    hidden = (jax.nn.silu(gate_pre.astype(F32)) * up_pre.astype(F32)).astype(BF16)
    summed = lax.psum_scatter(
        jnp.dot(hidden, down_weight, preferred_element_type=F32),
        "wide",
        scatter_dimension=0,
        tiled=True,
    )
    return summed.astype(BF16)


def kernel(
    steps, rows,
    gate_hbm, up_hbm, w_hbm, out_ref,
    gate, up, hidden, w_buf,
    c_send, c_recv, c_own, y_send, y_recv, y_own, z_send, z_recv, z_own,
    in_sem, w_sem, c_ssem, c_rsem, y_ssem, y_rsem, z_ssem, z_rsem,
):
    group = lax.axis_index("groups")
    me = lax.axis_index("wide")
    z, y, c = me // 4, (me // 2) % 2, me % 2

    def device(zz, yy, cc):
        return (group, zz * 4 + yy * 2 + cc)

    core_peer = device(z, y, 1 - c)
    y_peer = device(z, 1 - y, c)
    z_peers = [device(lax.rem(z + k, ZS), y, c) for k in range(1, ZS)]

    def w_copy(t):
        slot = lax.rem(t, SLOTS)
        return pltpu.make_async_copy(
            w_hbm.at[:, pl.ds(pl.multiple_of(t * CHUNK, CHUNK), CHUNK)], w_buf.at[slot], w_sem.at[slot]
        )

    def in_copies(p):
        a, b, k = p // (2 * ZS), (p // ZS) % 2, p % ZS
        owner = device(lax.rem(z + k, ZS), y if b else 1 - y, c if a else 1 - c)[1]
        src = pl.ds(pl.multiple_of(owner * rows, rows), rows)
        dst = pl.ds(p * rows, rows)
        return (
            pltpu.make_async_copy(gate_hbm.at[src], gate.at[dst], in_sem.at[0, p]),
            pltpu.make_async_copy(up_hbm.at[src], up.at[dst], in_sem.at[1, p]),
        )

    for p in range(WIDE):
        for copy in in_copies(p):
            copy.start()
    for t in range(SLOTS):
        w_copy(t).start()

    barrier = pltpu.get_barrier_semaphore()
    peers = [core_peer, y_peer] + z_peers
    for peer in peers:
        pl.semaphore_signal(barrier, inc=1, device_id=peer, device_id_type=MESH)

    for p in range(WIDE):
        for copy in in_copies(p):
            copy.wait()
        block = pl.ds(p * rows, rows)
        v = gate[block].astype(F32)
        hidden[block] = (v / (1.0 + jnp.exp(-v)) * up[block].astype(F32)).astype(BF16)

    pl.semaphore_wait(barrier, len(peers))

    def c_copy(t):
        return pltpu.make_async_remote_copy(
            c_send.at[t], c_recv.at[t], c_ssem.at[t], c_rsem.at[t], device_id=core_peer, device_id_type=MESH
        )

    def y_copy(t):
        return pltpu.make_async_remote_copy(
            y_send.at[t], y_recv.at[t], y_ssem.at[t], y_rsem.at[t], device_id=y_peer, device_id_type=MESH
        )

    def z_copy(k, t):
        return pltpu.make_async_remote_copy(
            z_send.at[k, t], z_recv.at[k, t], z_ssem.at[k, t], z_rsem.at[k, t],
            device_id=z_peers[k], device_id_type=MESH,
        )

    half, quarter = 8 * rows, 4 * rows

    def multiply(t):
        w_copy(t).wait()
        w = w_buf[lax.rem(t, SLOTS)]
        product = jnp.dot(hidden[...], w, preferred_element_type=F32)
        c_send[t] = product[:half].astype(BF16)
        c_own[t] = product[half:]
        c_copy(t).start()

        @pl.when(t + SLOTS < steps)
        def _():
            w_copy(t + SLOTS).start()

    def add_core(t):
        c_copy(t).wait_recv()
        y_send[t] = (c_own[t, :quarter] + c_recv[t, :quarter].astype(F32)).astype(BF16)
        y_copy(t).start()
        y_own[t] = c_own[t, quarter:] + c_recv[t, quarter:].astype(F32)

    def add_y(t):
        y_copy(t).wait_recv()
        for k in range(1, ZS):
            part = slice(k * rows, (k + 1) * rows)
            z_send[k - 1, t] = (y_own[t, part] + y_recv[t, part].astype(F32)).astype(BF16)
            z_copy(k - 1, t).start()
        z_own[t] = y_own[t, :rows] + y_recv[t, :rows].astype(F32)

    def add_z(t):
        total = z_own[t]
        for k in range(ZS - 1):
            z_copy(k, t).wait_recv()
            total += z_recv[k, t].astype(F32)
        out_ref[:, pl.ds(pl.multiple_of(t * CHUNK, CHUNK), CHUNK)] = total.astype(BF16)

    lags = (0, 1, 3, 6)
    stages = (multiply, add_core, add_y, add_z)

    def step(t, carry):
        for lag, stage in zip(lags, stages):
            @pl.when((t >= lag) & (t < steps + lag))
            def _(lag=lag, stage=stage):
                stage(t - lag)
        return carry

    lax.fori_loop(0, steps + lags[-1], step, 0)

    def drain(t, carry):
        c_copy(t).wait_send()
        y_copy(t).wait_send()
        for k in range(ZS - 1):
            z_copy(k, t).wait_send()
        return carry

    lax.fori_loop(0, steps, drain, 0)


def fused_per_device(gate_pre, up_pre, down_weight):
    tokens, depth = gate_pre.shape
    columns = down_weight.shape[1]
    rows, steps = tokens // WIDE, columns // CHUNK
    dma = pltpu.SemaphoreType.DMA
    return pl.pallas_call(
        functools.partial(kernel, steps, rows),
        out_shape=jax.ShapeDtypeStruct((rows, columns), BF16),
        in_specs=[pl.BlockSpec(memory_space=pl.ANY)] * 3,
        out_specs=pl.BlockSpec(memory_space=pltpu.VMEM),
        scratch_shapes=[
            pltpu.VMEM((tokens, depth), BF16),
            pltpu.VMEM((tokens, depth), BF16),
            pltpu.VMEM((tokens, depth), BF16),
            pltpu.VMEM((SLOTS, depth, CHUNK), BF16),
            pltpu.VMEM((steps, 8 * rows, CHUNK), BF16),
            pltpu.VMEM((steps, 8 * rows, CHUNK), BF16),
            pltpu.VMEM((steps, 8 * rows, CHUNK), F32),
            pltpu.VMEM((steps, 4 * rows, CHUNK), BF16),
            pltpu.VMEM((steps, 4 * rows, CHUNK), BF16),
            pltpu.VMEM((steps, 4 * rows, CHUNK), F32),
            pltpu.VMEM((ZS - 1, steps, rows, CHUNK), BF16),
            pltpu.VMEM((ZS - 1, steps, rows, CHUNK), BF16),
            pltpu.VMEM((steps, rows, CHUNK), F32),
            dma((2, WIDE)),
            dma((SLOTS,)),
            dma((steps,)),
            dma((steps,)),
            dma((steps,)),
            dma((steps,)),
            dma((ZS - 1, steps)),
            dma((ZS - 1, steps)),
        ],
        compiler_params=pltpu.CompilerParams(
            collective_id=0, has_side_effects=True, vmem_limit_bytes=60 * 2**20
        ),
        cost_estimate=pl.CostEstimate(
            flops=2 * tokens * depth * columns,
            bytes_accessed=2 * (2 * tokens * depth + depth * columns + rows * columns),
            transcendentals=tokens * depth,
        ),
    )(gate_pre, up_pre, down_weight)


def solution(mesh):
    in_specs = (P("groups", "wide"), P("groups", "wide"), P("wide", None))
    out_specs = P(("groups", "wide"), None)
    body = fused_per_device if mesh.shape["wide"] == WIDE else plain_per_device
    return jax.shard_map(body, mesh=mesh, in_specs=in_specs, out_specs=out_specs, check_vma=False)
```

```python
import functools

import jax
import jax.numpy as jnp
from jax import lax
from jax.experimental import pallas as pl
from jax.experimental.pallas import tpu as pltpu
from jax.sharding import PartitionSpec as P

MESH = pl.DeviceIdType.MESH
BF16 = jnp.bfloat16
F32 = jnp.float32

ZS = 4
WIDE = 4 * ZS
CHUNK = 512
SLOTS = 3
EVERY, B_CHUNKS = 5, 3
LAGS = (1, 4, 4, 7, 7, 10, 10)


def plain_per_device(gate_pre, up_pre, down_weight):
    hidden = (jax.nn.silu(gate_pre.astype(F32)) * up_pre.astype(F32)).astype(BF16)
    summed = lax.psum_scatter(
        jnp.dot(hidden, down_weight, preferred_element_type=F32),
        "wide",
        scatter_dimension=0,
        tiled=True,
    )
    return summed.astype(BF16)


def kernel(
    steps, rows,
    gate_hbm, up_hbm, w_hbm, out_ref,
    gate, up, hidden, w_buf,
    c_send, c_recv, c_own, y_send, y_recv, y_own, z_send, z_recv, z_own,
    bz_send, bz_recv, bz_own, by_send, by_recv, by_own,
    in_sem, w_sem, c_ssem, c_rsem, y_ssem, y_rsem, z_ssem, z_rsem,
):
    group = lax.axis_index("groups")
    me = lax.axis_index("wide")
    z, y, c = me // 4, (me // 2) % 2, me % 2
    zx = (z, z + 1 - 2 * (z % 2), (z + 2) % 4, 3 - z)
    edge = ((z + 1) // 2 + 1) % 2
    half, quarter = 8 * rows, 4 * rows

    def device(zz, yy, cc):
        return (group, zz * 4 + yy * 2 + cc)

    core_peer = device(z, y, 1 - c)
    y_peer = device(z, 1 - y, c)
    z_peers = [device(zx[k], y, c) for k in range(1, ZS)]

    def w_copy(t):
        slot = lax.rem(t, SLOTS)
        return pltpu.make_async_copy(
            w_hbm.at[:, pl.ds(pl.multiple_of(t * CHUNK, CHUNK), CHUNK)], w_buf.at[slot], w_sem.at[slot]
        )

    def in_copies(p):
        a, b, k = p // (2 * ZS), (p // ZS) % 2, p % ZS
        owner = device(zx[k], y if b else 1 - y, c if a else 1 - c)[1]
        src = pl.ds(pl.multiple_of(owner * rows, rows), rows)
        dst = pl.ds(p * rows, rows)
        return (
            pltpu.make_async_copy(gate_hbm.at[src], gate.at[dst], in_sem.at[0, p]),
            pltpu.make_async_copy(up_hbm.at[src], up.at[dst], in_sem.at[1, p]),
        )

    def activate(p):
        for copy in in_copies(p):
            copy.wait()
        block = pl.ds(p * rows, rows)
        v = gate[block].astype(F32)
        hidden[block] = (v / (1.0 + jnp.exp(-v)) * up[block].astype(F32)).astype(BF16)

    def c_copy(t):
        return pltpu.make_async_remote_copy(
            c_send.at[t], c_recv.at[t], c_ssem.at[t], c_rsem.at[t], device_id=core_peer, device_id_type=MESH
        )

    def y_copy(t, i, send, recv):
        return pltpu.make_async_remote_copy(
            send.at[i], recv.at[i], y_ssem.at[t], y_rsem.at[t], device_id=y_peer, device_id_type=MESH
        )

    def z_copy(k, t, i, send, recv):
        slot = 3 * (1 - edge) if k == 3 else k
        to = device(edge * zx[1] + (1 - edge) * zx[3], y, c) if k == 3 else z_peers[k - 1]
        return pltpu.make_async_remote_copy(
            send.at[k, i], recv.at[slot, i], z_ssem.at[k, t], z_rsem.at[slot, t], device_id=to, device_id_type=MESH
        )

    def z_arrival(slot, t, i, send, recv):
        return pltpu.make_async_remote_copy(
            send.at[1, i], recv.at[slot, i], z_ssem.at[1, t], z_rsem.at[slot, t],
            device_id=z_peers[0], device_id_type=MESH,
        )

    def z_start(t, i, send, recv, own, blocks):
        for k in (3, 1):
            send[k, i] = blocks(k).astype(BF16)
            z_copy(k, t, i, send, recv).start()

        @pl.when(edge == 1)
        def _():
            send[2, i] = blocks(2).astype(BF16)
            z_copy(2, t, i, send, recv).start()

        @pl.when(edge == 0)
        def _():
            own[1, i] = blocks(2)

        own[0, i] = blocks(0)

    def z_merge(t, i, send, recv, own):
        @pl.when(edge == 0)
        def _():
            z_arrival(0, t, i, send, recv).wait_recv()
            send[2, i] = (own[1, i] + recv[0, i].astype(F32)).astype(BF16)
            z_copy(2, t, i, send, recv).start()

    def z_finish(t, i, send, recv, own):
        @pl.when(edge == 0)
        def _():
            z_arrival(3, t, i, send, recv).wait_recv()
            own[0, i] = own[0, i] + recv[3, i].astype(F32)

        for k in (1, 2):
            z_arrival(k, t, i, send, recv).wait_recv()
        return own[0, i] + recv[1, i].astype(F32) + recv[2, i].astype(F32)

    a_z = (z_send, z_recv, z_own)
    b_z = (bz_send, bz_recv, bz_own)

    def store(t, total):
        out_ref[:, pl.ds(pl.multiple_of(t * CHUNK, CHUNK), CHUNK)] = total.astype(BF16)

    def multiply(t):
        w_copy(t).wait()
        product = jnp.dot(hidden[...], w_buf[lax.rem(t, SLOTS)], preferred_element_type=F32)
        c_send[t] = product[:half].astype(BF16)
        c_own[t] = product[half:]
        c_copy(t).start()

        @pl.when(t + SLOTS < steps)
        def _():
            w_copy(t + SLOTS).start()

    def core_sum(t, part):
        return c_own[t, part] + c_recv[t, part].astype(F32)

    def a_core(t):
        c_copy(t).wait_recv()
        y_send[t] = core_sum(t, slice(0, quarter)).astype(BF16)
        y_copy(t, t, y_send, y_recv).start()
        y_own[t] = core_sum(t, slice(quarter, half))

    def a_y(t):
        y_copy(t, t, y_send, y_recv).wait_recv()

        def blocks(k):
            part = slice(k * rows, (k + 1) * rows)
            return y_own[t, part] + y_recv[t, part].astype(F32)

        z_start(t, t, *a_z, blocks)

    def a_merge(t):
        z_merge(t, t, *a_z)

    def a_z_finish(t):
        store(t, z_finish(t, t, *a_z))

    def b_core(t):
        i = t // EVERY
        c_copy(t).wait_recv()

        def blocks(k):
            return jnp.concatenate(
                [core_sum(t, slice(p * rows, (p + 1) * rows)) for p in (k, ZS + k)], axis=0
            )

        z_start(t, i, *b_z, blocks)

    def b_merge(t):
        z_merge(t, t // EVERY, *b_z)

    def b_z_finish(t):
        i = t // EVERY
        total = z_finish(t, i, *b_z)
        by_send[i] = total[:rows].astype(BF16)
        y_copy(t, i, by_send, by_recv).start()
        by_own[i] = total[rows:]

    def b_y(t):
        i = t // EVERY
        y_copy(t, i, by_send, by_recv).wait_recv()
        store(t, by_own[i] + by_recv[i].astype(F32))

    def is_b(t):
        return (t % EVERY == 1) & (t // EVERY < B_CHUNKS)

    def is_a(t):
        return (t % EVERY != 1) | (t // EVERY >= B_CHUNKS)

    for p in range(WIDE // 2):
        for copy in in_copies(p):
            copy.start()
    w_copy(0).start()
    for p in range(WIDE // 2, WIDE):
        for copy in in_copies(p):
            copy.start()
    for t in range(1, SLOTS):
        w_copy(t).start()

    barrier = pltpu.get_barrier_semaphore()
    peers = [core_peer, y_peer] + z_peers
    for peer in peers:
        pl.semaphore_signal(barrier, inc=1, device_id=peer, device_id_type=MESH)

    for p in range(WIDE // 2):
        activate(p)
    w_copy(0).wait()
    c_send[0] = jnp.dot(hidden[:half], w_buf[0], preferred_element_type=F32).astype(BF16)
    pl.semaphore_wait(barrier, len(peers))
    c_copy(0).start()
    for p in range(WIDE // 2, WIDE):
        activate(p)
    c_own[0] = jnp.dot(hidden[half:], w_buf[0], preferred_element_type=F32)
    w_copy(SLOTS).start()

    schedule = (
        (LAGS[0], is_a, a_core),
        (LAGS[0], is_b, b_core),
        (LAGS[1], is_a, a_y),
        (LAGS[2], is_b, b_merge),
        (LAGS[3], is_a, a_merge),
        (LAGS[4], is_b, b_z_finish),
        (LAGS[5], is_a, a_z_finish),
        (LAGS[6], is_b, b_y),
    )

    def step(t, carry):
        @pl.when(t < steps)
        def _():
            multiply(t)

        for lag, kind, stage in schedule:
            @pl.when((t >= lag) & (t < steps + lag) & kind(t - lag))
            def _(lag=lag, stage=stage):
                stage(t - lag)
        return carry

    lax.fori_loop(1, steps + max(LAGS), step, 0)

    def drain(t, carry):
        c_copy(t).wait_send()

        @pl.when(is_a(t))
        def _():
            y_copy(t, t, y_send, y_recv).wait_send()
            for k in range(1, ZS):
                z_copy(k, t, t, z_send, z_recv).wait_send()

        @pl.when(is_b(t))
        def _():
            i = t // EVERY
            y_copy(t, i, by_send, by_recv).wait_send()
            for k in range(1, ZS):
                z_copy(k, t, i, bz_send, bz_recv).wait_send()

        return carry

    lax.fori_loop(0, steps, drain, 0)


def fused_per_device(gate_pre, up_pre, down_weight):
    tokens, depth = gate_pre.shape
    columns = down_weight.shape[1]
    rows, steps = tokens // WIDE, columns // CHUNK
    dma = pltpu.SemaphoreType.DMA
    vmem = pltpu.VMEM
    return pl.pallas_call(
        functools.partial(kernel, steps, rows),
        out_shape=jax.ShapeDtypeStruct((rows, columns), BF16),
        in_specs=[pl.BlockSpec(memory_space=pl.ANY)] * 3,
        out_specs=pl.BlockSpec(memory_space=pltpu.VMEM),
        scratch_shapes=[
            vmem((tokens, depth), BF16),
            vmem((tokens, depth), BF16),
            vmem((tokens, depth), BF16),
            vmem((SLOTS, depth, CHUNK), BF16),
            vmem((steps, 8 * rows, CHUNK), BF16),
            vmem((steps, 8 * rows, CHUNK), BF16),
            vmem((steps, 8 * rows, CHUNK), F32),
            vmem((steps, 4 * rows, CHUNK), BF16),
            vmem((steps, 4 * rows, CHUNK), BF16),
            vmem((steps, 4 * rows, CHUNK), F32),
            vmem((ZS, steps, rows, CHUNK), BF16),
            vmem((ZS, steps, rows, CHUNK), BF16),
            vmem((2, steps, rows, CHUNK), F32),
            vmem((ZS, B_CHUNKS, 2 * rows, CHUNK), BF16),
            vmem((ZS, B_CHUNKS, 2 * rows, CHUNK), BF16),
            vmem((2, B_CHUNKS, 2 * rows, CHUNK), F32),
            vmem((B_CHUNKS, rows, CHUNK), BF16),
            vmem((B_CHUNKS, rows, CHUNK), BF16),
            vmem((B_CHUNKS, rows, CHUNK), F32),
            dma((2, WIDE)),
            dma((SLOTS,)),
            dma((steps,)),
            dma((steps,)),
            dma((steps,)),
            dma((steps,)),
            dma((ZS, steps)),
            dma((ZS, steps)),
        ],
        compiler_params=pltpu.CompilerParams(
            collective_id=0, has_side_effects=True, vmem_limit_bytes=60 * 2**20
        ),
        cost_estimate=pl.CostEstimate(
            flops=2 * tokens * depth * columns,
            bytes_accessed=2 * (2 * tokens * depth + depth * columns + rows * columns),
            transcendentals=tokens * depth,
        ),
    )(gate_pre, up_pre, down_weight)


def solution(mesh):
    in_specs = (P("groups", "wide"), P("groups", "wide"), P("wide", None))
    out_specs = P(("groups", "wide"), None)
    body = fused_per_device if mesh.shape["wide"] == WIDE else plain_per_device
    return jax.shard_map(body, mesh=mesh, in_specs=in_specs, out_specs=out_specs, check_vma=False)
```
